256 devices in a mesh: dp: 4 (over y_lo, core), ctx: 64 (over z, x, y_hi).
Axes of the slice: x: 4, y: 4 (y_hi: 2, y_lo: 2; y = y_hi * 2 + y_lo), z: 8, core: 2. Of those that a mesh axis runs over, the one named last changes fastest.
Arguments:
- queries: bfloat16 [4, 16384, 4096], P('dp', 'ctx'), may hold values from -130 to 130
- keys: bfloat16 [4, 16384, 1024], P('dp', 'ctx'), may hold values from -5 to 5
- values: bfloat16 [4, 16384, 1024], P('dp', 'ctx'), may hold values from -6 to 6
- out_grad: bfloat16 [4, 16384, 4096], P('dp', 'ctx'), may hold values from -6 to 6
- layer_input: bfloat16 [4, 16384, 4096], P('dp', 'ctx'), may hold values from -16 to 16
- doc_lengths: int32 [4, 64], P('dp'), may hold values from 1 to 512, 16384 in all within a row
Outputs:
- query_grad: bfloat16 [4, 16384, 4096], P('dp', 'ctx')
- key_grad: bfloat16 [4, 16384, 1024], P('dp', 'ctx')
- value_grad: bfloat16 [4, 16384, 1024], P('dp', 'ctx')
- value_weight_grad: float32 [4096, 1024], P(('dp', 'ctx'))
The draws below stay inside these ranges and needn't reach their ends.
Inputs may be any that keep to these rules, and one draw needn't show every extreme that they name: `doc_lengths`: each sequence's lengths sum to 16384, and the longest document of each sequence has exactly 512 tokens.
All inputs are finite; a program needn't handle non-finite values.
Results may differ from the reference program's by a relative error of at most 0.029.
Values may be sent and summed in bfloat16 or wider, within the bound.
A program may use at most 128 MiB of HBM per device.

```python
import math
from functools import reduce
import jax
import jax.numpy as jnp
import numpy as np
from jax import lax

KVH = 8
HD = 128
TOK_DEV = 256
REACH = 2
D = 4096
KVW = 1024
GROUP = 4
TOKENS = 16384
DOCS = 64
N_DP = 4
N_CTX = 64


def base_keys(key):
    return jnp.clip(jax.random.normal(key, (N_DP, TOKENS, KVW), jnp.float32), -5.0, 5.0)


def draw_keys(key, part):
    shared = base_keys(key)
    return shared.astype(jnp.bfloat16)


def draw_queries(key, part):
    key = jax.random.fold_in(key, 5)
    own = jnp.clip(jax.random.normal(key, (N_DP, TOKENS, D), jnp.float32), -5.0, 5.0)
    return own.astype(jnp.bfloat16)


def with_spikes(entries, own_key, source, target, blocks, factor):
    def block_of(dim):
        return (jnp.arange(entries.shape[dim]) // (entries.shape[dim] // blocks)).reshape((-1,) + (1,) * (entries.ndim - 1 - dim))

    one_side = jax.random.permutation(own_key, blocks)[block_of(target)]
    far = (block_of(target) + blocks // 2) % blocks
    return jnp.where((block_of(source) == one_side) | (block_of(source) == far), factor * entries, entries)


def shard_levels(stream_key, dims, cuts, low, high):
    def one(dim, parts):
        steps = jax.random.uniform(jax.random.fold_in(jax.random.fold_in(stream_key, 6), dim), (parts,), jnp.float32, low / len(cuts), high / len(cuts))
        return jnp.repeat(jnp.exp(steps), dims[dim] // parts).reshape((-1,) + (1,) * (len(dims) - dim - 1))

    gain = one(*cuts[0])
    for cut in cuts[1:]:
        gain = gain * one(*cut)
    return gain


def length_profile(count, total, most, skew):
    portions = [(1 << 20) // math.isqrt(rank ** skew) + 1 for rank in range(2, count + 1)]
    spare, given = total - most - (count - 1), [1] * (count - 1)
    while spare > 0:
        movable = [i for i in range(count - 1) if given[i] < most]
        mass, left = sum([portions[i] for i in movable]), spare
        for i in movable:
            addition = min(most - given[i], max(1, left * portions[i] // mass), spare)
            given[i] = given[i] + addition
            spare = spare - addition
    return np.array([most] + given)


def uneven_parts(own_key, amount, total, limit, lean):
    if amount == 2:
        one = jax.random.randint(own_key, (), max(1, total - limit), min(limit, total - 1) + 1)
        return jnp.stack([one, total - one])
    tallies = jnp.asarray(length_profile(amount, total, limit, lean), jnp.int32)
    pairs = (amount - 1) // 2
    source_of, taker = tallies[1:1 + 2 * pairs:2], tallies[2:2 + 2 * pairs:2]
    margin = jnp.minimum(source_of - 1, limit - taker)
    moved = jax.random.randint(jax.random.fold_in(own_key, 1), (pairs,), 0, 1 << 20) % (margin + 1)
    tallies = tallies.at[1:1 + 2 * pairs:2].set(source_of - moved).at[2:2 + 2 * pairs:2].set(taker + moved)
    return tallies[jax.random.permutation(jax.random.fold_in(own_key, 2), amount)]


def normal_values(key, dims, spread, reach, cuts=(), kind=jnp.bfloat16):
    entries = jax.random.normal(key, dims, jnp.float32) * spread
    if len(cuts) > 0:
        entries = shard_levels(key, dims, cuts, -0.22, 0.18) * entries
    return jnp.clip(entries, min=-reach, max=reach).astype(kind)


def noise_with(own_key, extent, scale, reach, pieces, heavy, kind=jnp.bfloat16):
    array = scale * jax.random.normal(own_key, extent, jnp.float32)
    if pieces:
        array = array * shard_levels(own_key, extent, pieces, -0.22, 0.18)
    return jnp.clip(with_spikes(array, jax.random.fold_in(own_key, 3), *heavy), -reach, reach).astype(kind)


def setup_inputs(seed: int = 0) -> dict:
    seeds = jax.random.split(jax.random.key(seed), 7)
    return {
        "queries": draw_queries(jax.random.fold_in(seeds[6], 71), 0),
        "keys": draw_keys(jax.random.fold_in(seeds[6], 71), 0),
        "values": normal_values(seeds[2], (N_DP, TOKENS, KVW), 1.0, 6.0, ((0, 4), (1, 64))),
        "out_grad": normal_values(seeds[3], (N_DP, TOKENS, D), 1.0, 6.0, ((0, 4), (1, 64))),
        "layer_input": noise_with(seeds[4], (N_DP, TOKENS, D), 1.0, 16.0, ((0, 4), (1, 64)), (1, 2, 64, 4.0)),
        "doc_lengths": jax.vmap(lambda own: uneven_parts(own, DOCS, TOKENS, REACH * TOK_DEV, 2))(jax.random.split(seeds[5], N_DP)).reshape((N_DP, DOCS)).astype(jnp.int32),
    }


def slab_grads(q_slab, k_window, v_window, do_slab, mask):
    scale = HD ** -0.5
    qf = q_slab.astype(jnp.float32).reshape(-1, KVH, GROUP, HD)
    dof = do_slab.astype(jnp.float32).reshape(-1, KVH, GROUP, HD)
    kf = k_window.astype(jnp.float32).reshape(-1, KVH, HD)
    vf = v_window.astype(jnp.float32).reshape(-1, KVH, HD)
    scores = jnp.einsum('sged,wgd->gesw', qf, kf) * scale
    live = mask[None, None]
    top = jnp.max(jnp.where(live, scores, -1e30), axis=-1, keepdims=True)
    total = jnp.sum(jnp.where(live, jnp.exp(scores - top), 0.0), axis=-1, keepdims=True)
    lse = top + jnp.log(total)
    probs = jnp.where(live, jnp.exp(scores - lse), 0.0)
    probs_b = lax.optimization_barrier(probs.astype(jnp.bfloat16)).astype(jnp.float32)
    attn_out = jnp.einsum('gesw,wgd->sged', probs_b, vf)
    delta = jnp.transpose(jnp.sum(dof * attn_out, axis=-1), (1, 2, 0))[..., None]
    dprobs = jnp.einsum('sged,wgd->gesw', dof, vf)
    dscores_b = lax.optimization_barrier((probs * (dprobs - delta)).astype(jnp.bfloat16)).astype(jnp.float32)
    rows = q_slab.shape[0]
    width = k_window.shape[0]
    dq = (jnp.einsum('gesw,wgd->sged', dscores_b, kf) * scale).reshape(rows, D)
    dk = (jnp.einsum('gesw,sged->wgd', dscores_b, qf) * scale).reshape(width, KVW)
    dv = jnp.einsum('gesw,sged->wgd', probs_b, dof).reshape(width, KVW)
    return dq, dk, dv


def one_replica(inputs):
    queries, keys, values, out_grad, lengths = inputs
    ends = jnp.cumsum(lengths).astype(jnp.int32)
    starts = (ends - lengths).astype(jnp.int32)
    width = (REACH + 1) * TOK_DEV
    k_pad = jnp.concatenate([jnp.zeros((REACH * TOK_DEV, KVW), keys.dtype), keys], 0)
    v_pad = jnp.concatenate([jnp.zeros((REACH * TOK_DEV, KVW), values.dtype), values], 0)

    def step(carry, slab):
        dk_acc, dv_acc = carry
        first = (slab * TOK_DEV).astype(jnp.int32)
        qpos = first + jnp.arange(TOK_DEV, dtype=jnp.int32)
        kpos = first - REACH * TOK_DEV + jnp.arange(width, dtype=jnp.int32)
        qstart = jnp.max(jnp.where(starts[None, :] <= qpos[:, None], starts[None, :], 0), axis=1)
        mask = (kpos[None, :] <= qpos[:, None]) & (kpos[None, :] >= qstart[:, None])
        q_slab = lax.dynamic_slice_in_dim(queries, first, TOK_DEV, 0)
        do_slab = lax.dynamic_slice_in_dim(out_grad, first, TOK_DEV, 0)
        k_window = lax.dynamic_slice_in_dim(k_pad, first, width, 0)
        v_window = lax.dynamic_slice_in_dim(v_pad, first, width, 0)
        dq, dk, dv = slab_grads(q_slab, k_window, v_window, do_slab, mask)
        dk_acc = lax.dynamic_update_slice_in_dim(dk_acc, lax.dynamic_slice_in_dim(dk_acc, first, width, 0) + dk, first, 0)
        dv_acc = lax.dynamic_update_slice_in_dim(dv_acc, lax.dynamic_slice_in_dim(dv_acc, first, width, 0) + dv, first, 0)
        return (dk_acc, dv_acc), dq.astype(jnp.bfloat16)

    zeros = jnp.zeros(((N_CTX + REACH) * TOK_DEV, KVW), jnp.float32)
    (dk_acc, dv_acc), dq = lax.scan(step, (zeros, zeros), jnp.arange(N_CTX, dtype=jnp.int32))
    return (dq.reshape(TOKENS, D), dk_acc[REACH * TOK_DEV:].astype(jnp.bfloat16),
            dv_acc[REACH * TOK_DEV:].astype(jnp.bfloat16))


def reference(queries, keys, values, out_grad, layer_input, doc_lengths):
    query_grad, key_grad, value_grad = lax.map(one_replica, (queries, keys, values, out_grad, doc_lengths))
    terms = [jnp.dot(layer_input[b].T, value_grad[b], preferred_element_type=jnp.float32) for b in range(N_DP)]
    value_weight_grad = reduce(lambda left, right: left + right, terms)
    return query_grad, key_grad, value_grad, value_weight_grad
```

```python
import jax
import jax.numpy as jnp
from jax import lax
from jax.experimental import pallas as pl
from jax.experimental.pallas import tpu as pltpu
from jax.sharding import PartitionSpec as P

KVH = 8
HD = 128
REACH = 2
GROUP = 4


def shifted(block, axis, distance):
    devices = range(lax.axis_size(axis))
    route = [(i - distance, i) for i in devices if i - distance in devices]
    return lax.ppermute(block, axis, route)


def group_grads(group, carry, q_rows, k_window, v_window, do_rows, mask):
    dq_acc, dk_acc, dv_acc = carry
    scale = HD ** (-0.5)
    rows = q_rows.shape[0]
    q_group = lax.dynamic_slice_in_dim(q_rows, group * (GROUP * HD), GROUP * HD, 1).reshape(
        rows, GROUP, HD
    )
    do_group = lax.dynamic_slice_in_dim(do_rows, group * (GROUP * HD), GROUP * HD, 1).reshape(
        rows, GROUP, HD
    )
    k_group = lax.dynamic_slice_in_dim(k_window, group * HD, HD, 1)
    v_group = lax.dynamic_slice_in_dim(v_window, group * HD, HD, 1)
    scores = jnp.einsum("sed,wd->esw", q_group, k_group, preferred_element_type=jnp.float32) * scale
    live = mask[None]
    top = jnp.max(jnp.where(live, scores, -1e30), axis=-1, keepdims=True)
    total = jnp.sum(jnp.where(live, jnp.exp(scores - top), 0.0), axis=-1, keepdims=True)
    lse = top + jnp.log(total)
    probs = jnp.where(live, jnp.exp(scores - lse), 0.0)
    probs_b = probs.astype(jnp.bfloat16)
    attn_out = jnp.einsum("esw,wd->sed", probs_b, v_group, preferred_element_type=jnp.float32)
    delta = jnp.transpose(jnp.sum(do_group.astype(jnp.float32) * attn_out, axis=-1))[..., None]
    dprobs = jnp.einsum("sed,wd->esw", do_group, v_group, preferred_element_type=jnp.float32)
    dscores_b = (probs * (dprobs - delta)).astype(jnp.bfloat16)
    dq_group = (
        jnp.einsum("esw,wd->sed", dscores_b, k_group, preferred_element_type=jnp.float32) * scale
    )
    dk_group = (
        jnp.einsum("esw,sed->wd", dscores_b, q_group, preferred_element_type=jnp.float32) * scale
    )
    dv_group = jnp.einsum("esw,sed->wd", probs_b, do_group, preferred_element_type=jnp.float32)
    dq_acc = lax.dynamic_update_slice_in_dim(
        dq_acc, dq_group.reshape(rows, GROUP * HD), group * (GROUP * HD), 1
    )
    dk_acc = lax.dynamic_update_slice_in_dim(dk_acc, dk_group, group * HD, 1)
    dv_acc = lax.dynamic_update_slice_in_dim(dv_acc, dv_group, group * HD, 1)
    return (dq_acc, dk_acc, dv_acc)


def local(queries, keys, values, out_grad, layer_input, doc_lengths):
    q_rows = queries[0]
    k_rows = keys[0]
    v_rows = values[0]
    do_rows = out_grad[0]
    x_rows = layer_input[0]
    lengths = doc_lengths[0]
    rows = q_rows.shape[0]
    width = (REACH + 1) * rows
    here = lax.axis_index("ctx")
    ends = jnp.cumsum(lengths)
    starts = ends - lengths
    qpos = here * rows + jnp.arange(rows, dtype=jnp.int32)
    kpos = (here - REACH) * rows + jnp.arange(width, dtype=jnp.int32)
    qstart = jnp.max(jnp.where(starts[None, :] <= qpos[:, None], starts[None, :], 0), axis=1)
    mask = (kpos[None, :] <= qpos[:, None]) & (kpos[None, :] >= qstart[:, None])
    own_pair = jnp.stack((k_rows, v_rows))
    remote = [shifted(own_pair, "ctx", step) for step in range(1, REACH + 1)]
    ordered = [remote[REACH - 1 - index] for index in range(REACH)] + [own_pair]
    k_window = jnp.concatenate([pair[0] for pair in ordered], 0)
    v_window = jnp.concatenate([pair[1] for pair in ordered], 0)
    start_carry = (
        jnp.zeros((rows, q_rows.shape[1]), jnp.float32),
        jnp.zeros((width, k_rows.shape[1]), jnp.float32),
        jnp.zeros((width, k_rows.shape[1]), jnp.float32),
    )

    def loop_body(group, carry):
        return group_grads(group, carry, q_rows, k_window, v_window, do_rows, mask)

    dq_acc, dk_window, dv_window = lax.fori_loop(0, KVH, loop_body, start_carry)
    pieces = [
        jnp.stack(
            (
                dk_window[(REACH - step) * rows : (REACH - step + 1) * rows],
                dv_window[(REACH - step) * rows : (REACH - step + 1) * rows],
            )
        )
        for step in range(REACH + 1)
    ]
    summed = pieces[0]
    for step in range(1, REACH + 1):
        summed = summed + shifted(pieces[step], "ctx", -step)
    query_grad = dq_acc.astype(jnp.bfloat16)[None]
    key_grad = summed[0].astype(jnp.bfloat16)
    value_grad = summed[1].astype(jnp.bfloat16)
    value_weight_grad = weight_grad(x_rows, value_grad)
    return (query_grad, key_grad[None], value_grad[None], value_weight_grad)


MESH = pl.DeviceIdType.MESH
GROUPS = ((0, 256, "z"), (256, 256, "x"), (512, 256, "z"), (768, 256, "x"))


def place():
    dp, ctx = lax.axis_index("dp"), lax.axis_index("ctx")
    return {
        "core": lax.rem(dp, 2),
        "y": lax.rem(ctx, 2) * 2 + dp // 2,
        "x": lax.rem(ctx // 2, 4),
        "z": ctx // 8,
    }


def at(here, axis=None, step=0):
    spot = dict(here)
    if axis is not None:
        size = {"core": 2, "y": 4, "x": 4, "z": 8}[axis]
        spot[axis] = lax.rem(spot[axis] + (step + size), size)
    dp = lax.rem(spot["y"], 2) * 2 + spot["core"]
    ctx = spot["z"] * 8 + spot["x"] * 2 + spot["y"] // 2
    return (dp, ctx)


def greet(targets):
    barrier = pltpu.get_barrier_semaphore()
    for target in targets:
        pl.semaphore_signal(barrier, inc=1, device_id=target, device_id_type=MESH)
    pl.semaphore_wait(barrier, len(targets))


def push(src, dst, sems, slot, target):
    copy = pltpu.make_async_remote_copy(
        src_ref=src,
        dst_ref=dst,
        send_sem=sems.at[0, slot],
        recv_sem=sems.at[1, slot],
        device_id=target,
        device_id_type=MESH,
    )
    copy.start()
    return copy


def ring(here, axis, term, keep, width, out, inn, sems, base):
    size = {"x": 4, "z": 8}[axis]
    half = size // 2
    mid = width // 2
    total_of = lambda step: lax.rem(here[axis] + step + size, size)
    plus, minus = at(here, axis, 1), at(here, axis, -1)
    copies = [[], []]
    far = term(total_of(half)).astype(jnp.bfloat16)
    out[0, 0, :, :mid] = far[:, :mid]
    out[1, 0, :, mid:] = far[:, mid:]
    copies[0].append(push(out.at[0, 0, :, pl.ds(0, mid)], inn.at[0, 0, :, pl.ds(0, mid)], sems, base, plus))
    copies[1].append(push(out.at[1, 0, :, pl.ds(mid, mid)], inn.at[1, 0, :, pl.ds(mid, mid)], sems, base + 1, minus))
    yield
    for step in range(1, half):
        for way, (sign, target) in enumerate(((1, plus), (-1, minus))):
            mine = term(total_of(sign * (half - step)))
            copies[way][-1].wait_recv()
            if step == 1:
                got = slice(0, mid) if way == 0 else slice(mid, width)
                rest = slice(mid, width) if way == 0 else slice(0, mid)
                out[way, step, :, got] = (mine[:, got] + inn[way, 0, :, got].astype(jnp.float32)).astype(jnp.bfloat16)
                out[way, step, :, rest] = mine[:, rest].astype(jnp.bfloat16)
            else:
                out[way, step] = (mine + inn[way, step - 1].astype(jnp.float32)).astype(jnp.bfloat16)
            copies[way].append(push(out.at[way, step], inn.at[way, step], sems, base + 2 * step + way, target))
        yield
    mine = term(here[axis])
    copies[0][-1].wait_recv()
    copies[1][-1].wait_recv()
    keep(mine + inn[0, half - 1].astype(jnp.float32) + inn[1, half - 1].astype(jnp.float32))
    for way in copies:
        for copy in way:
            copy.wait_send()
    yield


def scatter_group(here, xt, dvg, out_ref, c0, width, first, big_out, big_in, small_out, small_in, mid_sum, low_sum, y_out, y_in, sems):
    def product(index):
        if first == "z":
            rows = xt[:, index].reshape(256, 512)
        else:
            rows = xt[:, :, index].reshape(512, 512)
        return jnp.dot(rows, dvg[:, c0 : c0 + width], preferred_element_type=jnp.float32)

    def keep_mid(value):
        mid_sum[...] = value.reshape(mid_sum.shape)

    def keep_low(value):
        low_sum[...] = value.reshape(low_sum.shape)

    second = "x" if first == "z" else "z"
    yield from ring(here, first, product, keep_mid, width, big_out, big_in, sems, 0)
    yield from ring(here, second, lambda index: mid_sum[:, index].reshape(64, width), keep_low, width, small_out, small_in, sems, 8)
    copies = []
    for step in range(1, 4):
        target = lax.rem(here["y"] + step, 4)
        y_out[step - 1] = low_sum[lax.rem(target, 2), target // 2].astype(jnp.bfloat16)
        copies.append(push(y_out.at[step - 1], y_in.at[step - 1], sems, 16 + step, at(here, "y", step)))
    yield
    value = low_sum[lax.rem(here["y"], 2), here["y"] // 2]
    for step in range(1, 4):
        copies[step - 1].wait_recv()
        value = value + y_in[step - 1].astype(jnp.float32)
    out_ref[:, c0 : c0 + width] = value
    for copy in copies:
        copy.wait_send()


def weight_kernel(x_ref, dv_ref, out_ref, xrecv, dvg, xt, pair_sems, *scratch):
    here = place()
    greet([at(here, "core", 1), at(here, "z", 1), at(here, "z", -1), at(here, "x", 1), at(here, "x", -1),
           at(here, "y", 1), at(here, "y", 2), at(here, "y", 3)])
    partner = at(here, "core", 1)
    mine, other = here["core"] * 1024, (1 - here["core"]) * 1024
    swaps = [push(dv_ref, dvg.at[pl.ds(256, 256)], pair_sems, 2, partner)]
    for part in range(2):
        columns = pl.ds(pl.multiple_of(part * 2048 + other, 128), 1024)
        swaps.append(push(x_ref.at[:, columns], xrecv.at[:, pl.ds(part * 1024, 1024)], pair_sems, part, partner))
    dvg[0:256] = dv_ref[...]
    for part in range(2):
        def own(z, carry):
            columns = pl.ds(pl.multiple_of(part * 2048 + mine + z * 128, 128), 128)
            xt[part, z, :, :, 0:256] = x_ref[:, columns].T.reshape(4, 32, 256)
            return carry
        lax.fori_loop(0, 8, own, 0)
    for swap in swaps:
        swap.wait()
    for part in range(2):
        def got(z, carry):
            columns = pl.ds(pl.multiple_of(part * 1024 + z * 128, 128), 128)
            xt[part, z, :, :, 256:512] = xrecv[:, columns].T.reshape(4, 32, 256)
            return carry
        lax.fori_loop(0, 8, got, 0)
    per = len(scratch) // len(GROUPS)
    running = [
        scatter_group(here, xt, dvg, out_ref, c0, width, first, *scratch[i * per : (i + 1) * per])
        for i, (c0, width, first) in enumerate(GROUPS)
    ]
    while running:
        alive = []
        for group in running:
            if next(group, "end") != "end":
                alive.append(group)
        running = alive


def group_scratch(width, first):
    big, small, span = ((4, 256), (2, 64), (2, 4, 32)) if first == "z" else ((2, 512), (4, 64), (2, 8, 32))
    return [
        pltpu.VMEM((2, *big, width), jnp.bfloat16),
        pltpu.VMEM((2, *big, width), jnp.bfloat16),
        pltpu.VMEM((2, *small, width), jnp.bfloat16),
        pltpu.VMEM((2, *small, width), jnp.bfloat16),
        pltpu.VMEM((*span, width), jnp.float32),
        pltpu.VMEM((2, 2, 16, width), jnp.float32),
        pltpu.VMEM((3, 16, width), jnp.bfloat16),
        pltpu.VMEM((3, 16, width), jnp.bfloat16),
        pltpu.SemaphoreType.DMA((2, 20)),
    ]


def weight_grad(x_rows, dv_rows):
    scratch = [
        pltpu.VMEM((256, 2048), jnp.bfloat16),
        pltpu.VMEM((512, 1024), jnp.bfloat16),
        pltpu.VMEM((2, 8, 4, 32, 512), jnp.bfloat16),
        pltpu.SemaphoreType.DMA((2, 3)),
    ]
    for _, width, first in GROUPS:
        scratch += group_scratch(width, first)
    return pl.pallas_call(
        weight_kernel,
        out_shape=jax.ShapeDtypeStruct((16, 1024), jnp.float32),
        in_specs=[pl.BlockSpec(memory_space=pltpu.VMEM)] * 2,
        out_specs=pl.BlockSpec(memory_space=pltpu.VMEM),
        scratch_shapes=scratch,
        compiler_params=pltpu.CompilerParams(
            collective_id=1, has_side_effects=True, vmem_limit_bytes=48 * 2**20
        ),
        cost_estimate=pl.CostEstimate(flops=2 * 256 * 4096 * 1024, bytes_accessed=8 * 2**20, transcendentals=0),
    )(x_rows, dv_rows)


def solution(mesh):
    placed = (
        P("dp", "ctx", None),
        P("dp", "ctx", None),
        P("dp", "ctx", None),
        P("dp", "ctx", None),
        P("dp", "ctx", None),
        P("dp", None),
    )
    return jax.shard_map(
        local,
        mesh=mesh,
        in_specs=placed,
        out_specs=(
            P("dp", "ctx", None),
            P("dp", "ctx", None),
            P("dp", "ctx", None),
            P(("dp", "ctx"), None),
        ),
        check_vma=False,
    )
```

```python
import jax
import jax.numpy as jnp
from jax import lax
from jax.experimental import pallas as pl
from jax.experimental.pallas import tpu as pltpu
from jax.sharding import PartitionSpec as P

KVH = 8
HD = 128
GROUP = 4
RS_FROM = 20
RS_EVERY = 0
MESH = pl.DeviceIdType.MESH
GROUPS = ((0, 256, "z"), (256, 256, "x"), (512, 256, "z"), (768, 256, "x"))


def place():
    dp, ctx = lax.axis_index("dp"), lax.axis_index("ctx")
    return {
        "core": lax.rem(dp, 2),
        "y": lax.rem(ctx, 2) * 2 + dp // 2,
        "x": lax.rem(ctx // 2, 4),
        "z": ctx // 8,
    }


def at(here, axis=None, step=0):
    spot = dict(here)
    if axis is not None:
        size = {"core": 2, "y": 4, "x": 4, "z": 8}[axis]
        spot[axis] = lax.rem(spot[axis] + (step + size), size)
    dp = lax.rem(spot["y"], 2) * 2 + spot["core"]
    ctx = spot["z"] * 8 + spot["x"] * 2 + spot["y"] // 2
    return (dp, ctx)


def greet(targets):
    barrier = pltpu.get_barrier_semaphore()
    for target in targets:
        pl.semaphore_signal(barrier, inc=1, device_id=target, device_id_type=MESH)
    pl.semaphore_wait(barrier, len(targets))


def push(src, dst, sems, slot, target):
    copy = pltpu.make_async_remote_copy(
        src_ref=src,
        dst_ref=dst,
        send_sem=sems.at[0, slot],
        recv_sem=sems.at[1, slot],
        device_id=target,
        device_id_type=MESH,
    )
    copy.start()
    return copy


def ring(here, axis, term, keep, width, out, inn, sems, base):
    size = {"x": 4, "z": 8}[axis]
    half = size // 2
    mid = width // 2
    total_of = lambda step: lax.rem(here[axis] + step + size, size)
    plus, minus = at(here, axis, 1), at(here, axis, -1)
    copies = [[], []]
    far = term(total_of(half)).astype(jnp.bfloat16)
    out[0, 0, :, :mid] = far[:, :mid]
    out[1, 0, :, mid:] = far[:, mid:]
    copies[0].append(push(out.at[0, 0, :, pl.ds(0, mid)], inn.at[0, 0, :, pl.ds(0, mid)], sems, base, plus))
    copies[1].append(push(out.at[1, 0, :, pl.ds(mid, mid)], inn.at[1, 0, :, pl.ds(mid, mid)], sems, base + 1, minus))
    yield
    for step in range(1, half):
        for way, (sign, target) in enumerate(((1, plus), (-1, minus))):
            mine = term(total_of(sign * (half - step)))
            copies[way][-1].wait_recv()
            if step == 1:
                got = slice(0, mid) if way == 0 else slice(mid, width)
                rest = slice(mid, width) if way == 0 else slice(0, mid)
                out[way, step, :, got] = (mine[:, got] + inn[way, 0, :, got].astype(jnp.float32)).astype(jnp.bfloat16)
                out[way, step, :, rest] = mine[:, rest].astype(jnp.bfloat16)
            else:
                out[way, step] = (mine + inn[way, step - 1].astype(jnp.float32)).astype(jnp.bfloat16)
            copies[way].append(push(out.at[way, step], inn.at[way, step], sems, base + 2 * step + way, target))
        yield
    mine = term(here[axis])
    copies[0][-1].wait_recv()
    copies[1][-1].wait_recv()
    keep(mine + inn[0, half - 1].astype(jnp.float32) + inn[1, half - 1].astype(jnp.float32))
    for way in copies:
        for copy in way:
            copy.wait_send()
    yield


def scatter_group(here, xt, dvg, out_ref, c0, width, first, big_out, big_in, small_out, small_in, mid_sum, low_sum, y_out, y_in, sems):
    def product(index):
        if first == "z":
            rows = xt[:, index].reshape(256, 512)
        else:
            rows = xt[:, :, index].reshape(512, 512)
        return jnp.dot(rows, dvg[:, c0 : c0 + width], preferred_element_type=jnp.float32)

    def keep_mid(value):
        mid_sum[...] = value.reshape(mid_sum.shape)

    def keep_low(value):
        low_sum[...] = value.reshape(low_sum.shape)

    second = "x" if first == "z" else "z"
    yield from ring(here, first, product, keep_mid, width, big_out, big_in, sems, 0)
    yield from ring(here, second, lambda index: mid_sum[:, index].reshape(64, width), keep_low, width, small_out, small_in, sems, 8)
    copies = []
    for step in range(1, 4):
        target = lax.rem(here["y"] + step, 4)
        y_out[step - 1] = low_sum[lax.rem(target, 2), target // 2].astype(jnp.bfloat16)
        copies.append(push(y_out.at[step - 1], y_in.at[step - 1], sems, 16 + step, at(here, "y", step)))
    yield
    value = low_sum[lax.rem(here["y"], 2), here["y"] // 2]
    for step in range(1, 4):
        copies[step - 1].wait_recv()
        value = value + y_in[step - 1].astype(jnp.float32)
    out_ref[:, c0 : c0 + width] = value
    for copy in copies:
        copy.wait_send()


def group_scratch(width, first):
    big, small, span = ((4, 256), (2, 64), (2, 4, 32)) if first == "z" else ((2, 512), (4, 64), (2, 8, 32))
    return [
        pltpu.VMEM((2, *big, width), jnp.bfloat16),
        pltpu.VMEM((2, *big, width), jnp.bfloat16),
        pltpu.VMEM((2, *small, width), jnp.bfloat16),
        pltpu.VMEM((2, *small, width), jnp.bfloat16),
        pltpu.VMEM((*span, width), jnp.float32),
        pltpu.VMEM((2, 2, 16, width), jnp.float32),
        pltpu.VMEM((3, 16, width), jnp.bfloat16),
        pltpu.VMEM((3, 16, width), jnp.bfloat16),
        pltpu.SemaphoreType.DMA((2, 20)),
    ]


SPAN = 640
HALF = 128
SCALE = HD ** (-0.5)
BF = jnp.bfloat16
F32 = jnp.float32


def dot_nt(left, right):
    return lax.dot_general(left, right, (((1,), (1,)), ((), ())), preferred_element_type=F32)


def dot_nn(left, right):
    return jnp.dot(left, right, preferred_element_type=F32)


def head_columns(head, count=1):
    return pl.ds(pl.multiple_of(head * HD, HD), count * HD)


def stacked(ref, g, half):
    rows = pl.ds(half * HALF, HALF)
    return jnp.concatenate([ref[rows, head_columns(g * GROUP + e)] for e in range(GROUP)], axis=0)


def fill_bias(lengths_ref, slab, bias):
    row = lax.broadcasted_iota(jnp.int32, (64, 64), 0)
    col = lax.broadcasted_iota(jnp.int32, (64, 64), 1)
    sizes = jnp.broadcast_to(lengths_ref[...], (64, 64))
    starts = jnp.sum(jnp.where(col < row, sizes, 0), axis=1, keepdims=True)
    for half in range(2):
        base = slab * 256 + half * HALF
        query = base + lax.broadcasted_iota(jnp.int32, (64, HALF), 1)
        first = jnp.max(jnp.where(starts <= query, starts, 0), axis=0, keepdims=True)
        key = base - 512 + lax.broadcasted_iota(jnp.int32, (SPAN, HALF), 0)
        query = base + lax.broadcasted_iota(jnp.int32, (SPAN, HALF), 1)
        value = jnp.where((key <= query) & (key >= first), 0.0, -1e30)
        for e in range(GROUP):
            bias[half, :, e * HALF : (e + 1) * HALF] = value


def probs_step(g, q_ref, do_ref, kwin, bias, pbuf, dvwin):
    for half in range(2):
        rows = pl.ds(half * HALF, SPAN)
        scores = dot_nt(kwin[g, rows], stacked(q_ref, g, half)) * (SCALE * 1.4426950408889634) + bias[half]
        top = jnp.max(scores, axis=0, keepdims=True)
        weights = jnp.exp2(scores - top)
        probs = (weights * (1.0 / jnp.sum(weights, axis=0, keepdims=True))).astype(BF)
        pbuf[g, half] = probs
        term = dot_nn(probs, stacked(do_ref, g, half))
        if half == 0:
            dvwin[0:SPAN] = term
            dvwin[SPAN:768] = jnp.zeros((HALF, HD), F32)
        else:
            dvwin[rows] += term


def grads_step(g, q_ref, do_ref, kwin, vwin, pbuf, dkwin, dq_ref):
    turned = kwin[g].T
    for half in range(2):
        rows = pl.ds(half * HALF, SPAN)
        probs = pbuf[g, half].astype(F32)
        dprobs = dot_nt(vwin[g, rows], stacked(do_ref, g, half))
        delta = jnp.sum(probs * dprobs, axis=0, keepdims=True)
        dscores = (probs * (dprobs - delta)).astype(BF)
        term = dot_nn(dscores, stacked(q_ref, g, half))
        if half == 0:
            dkwin[0:SPAN] = term
            dkwin[SPAN:768] = jnp.zeros((HALF, HD), F32)
        else:
            dkwin[rows] += term
        dq = dot_nn(turned[:, half * HALF : half * HALF + SPAN], dscores) * SCALE
        for e in range(GROUP):
            dq_ref[pl.ds(half * HALF, HALF), head_columns(g * GROUP + e)] = dq[:, e * HALF : (e + 1) * HALF].T.astype(BF)


LEAD = 3


def fused_kernel(lengths_ref, q_ref, k_ref, v_ref, do_ref, x_ref, dq_ref, dk_ref, dv_ref, dw_ref,
                 kwin, vwin, bias, pbuf, window, out1, in1, out2, in2, final, xrecv, dvg, xt, halo_sems, pair_sems, *scratch):
    here = place()
    dp, ctx = lax.axis_index("dp"), lax.axis_index("ctx")
    odd = lax.rem(ctx, 2)
    twin = (dp, ctx + 1 - 2 * odd)
    ahead, behind = (dp, lax.rem(ctx + 2, 64)), (dp, lax.rem(ctx + 62, 64))
    partner = at(here, "core", 1)
    relay = pl.multiple_of(512 * (1 - odd), 256)

    def link(src, dst, kind, g, target):
        return pltpu.make_async_remote_copy(
            src_ref=src, dst_ref=dst, send_sem=halo_sems.at[0, kind, g], recv_sem=halo_sems.at[1, kind, g],
            device_id=target, device_id_type=MESH)

    def halo_x(which, g):
        win = (kwin, vwin)[which]
        return link(win.at[g, pl.ds(512, 256)], win.at[g, pl.ds(0, 256)], 2 * which, g, ahead)

    def halo_y(which, g):
        win = (kwin, vwin)[which]
        return link(win.at[g, pl.ds(relay, 256)], win.at[g, pl.ds(256, 256)], 2 * which + 1, g, twin)

    def back_y(which, g):
        return link(out1.at[which, g], in1.at[which, g], 4 + 2 * which, g, twin)

    def back_x(which, g):
        return link(out2.at[which, g], in2.at[which, g], 5 + 2 * which, g, behind)

    def forward(which, g):
        halo_x(which, g).wait_recv()
        halo_y(which, g).start()

    def give_near(which, g):
        out1[which, g] = window[256:512].astype(BF)
        final[which, g] = window[512:768]
        out2[which, g] = window[0:256].astype(BF)
        back_y(which, g).start()

    def give_far(which, g):
        back_y(which, g).wait_recv()
        got = in1[which, g].astype(F32)
        out2[which, g] = (out2[which, g].astype(F32) + jnp.where(odd == 1, got, 0.0)).astype(BF)
        final[which, g] += jnp.where(odd == 1, 0.0, got)
        back_x(which, g).start()

    def finish(which, g):
        back_x(which, g).wait_recv()
        total = final[which, g] + in2[which, g].astype(F32)
        if which == 0:
            dk_ref[:, head_columns(g)] = (total * SCALE).astype(BF)
        else:
            rounded = total.astype(BF)
            dv_ref[:, head_columns(g)] = rounded
            dvg[0:256, head_columns(g)] = rounded

    swaps = []

    def share(g):
        columns = pl.ds(g * HD, 2 * HD)
        swaps.append(push(dvg.at[pl.ds(0, 256), columns], dvg.at[pl.ds(256, 256), columns], pair_sems, 2 + g // 2, partner))

    for g in range(KVH):
        kwin[g, 512:768] = k_ref[:, g * HD : (g + 1) * HD]
        vwin[g, 512:768] = v_ref[:, g * HD : (g + 1) * HD]
    greet([partner, at(here, "z", 1), at(here, "z", -1), at(here, "x", 1), at(here, "x", -1),
           at(here, "y", 1), at(here, "y", 2), at(here, "y", 3), ahead, behind])
    for which in range(2):
        for g in range(KVH):
            halo_x(which, g).start()
    mine, other = here["core"] * 1024, (1 - here["core"]) * 1024
    for part in range(2):
        columns = pl.ds(pl.multiple_of(part * 2048 + other, 128), 1024)
        swaps.append(push(x_ref.at[:, columns], xrecv.at[:, pl.ds(part * 1024, 1024)], pair_sems, part, partner))
    fill_bias(lengths_ref, ctx, bias)
    for g in range(LEAD):
        forward(0, g)
    for part in range(2):
        def own(z, carry):
            columns = pl.ds(pl.multiple_of(part * 2048 + mine + z * 128, 128), 128)
            xt[part, z, :, :, 0:256] = x_ref[:, columns].T.reshape(4, 32, 256)
            return carry
        lax.fori_loop(0, 8, own, 0)

    def tail(which, tick):
        if 0 <= tick - 2 < KVH:
            give_far(which, tick - 2)
        if 0 <= tick - 4 < KVH:
            finish(which, tick - 4)
            if which == 1 and (tick - 4) % 2 == 1:
                share(tick - 5)

    groups = []
    values_late = {5: (0,), 6: (1, 2), 7: (3, 4), 8: (5, 6), 9: (7,)}
    per = len(scratch) // len(GROUPS)
    for tick in range(2 * KVH + 5):
        for g in values_late.get(tick, ()):
            forward(1, g)
        if tick + LEAD < KVH:
            forward(0, tick + LEAD)
        if tick < KVH:
            halo_y(0, tick).wait_recv()
            probs_step(tick, q_ref, do_ref, kwin, bias, pbuf, window)
            give_near(1, tick)
        elif tick < 2 * KVH:
            halo_y(1, tick - KVH).wait_recv()
            grads_step(tick - KVH, q_ref, do_ref, kwin, vwin, pbuf, window, dq_ref)
            give_near(0, tick - KVH)
        tail(1, tick)
        tail(0, tick - KVH)
        if tick == 7:
            swaps[0].wait()
            swaps[1].wait()
            for part in range(2):
                def got(z, carry):
                    columns = pl.ds(pl.multiple_of(part * 1024 + z * 128, 128), 128)
                    xt[part, z, :, :, 256:512] = xrecv[:, columns].T.reshape(4, 32, 256)
                    return carry
                lax.fori_loop(0, 8, got, 0)
        for i, (c0, width, first) in enumerate(GROUPS):
            if tick == RS_FROM + RS_EVERY * i:
                swaps[2 + i].wait()
                groups.append(scatter_group(here, xt, dvg, dw_ref, c0, width, first, *scratch[i * per : (i + 1) * per]))
        groups = [group for group in groups if next(group, "end") != "end"]
    while groups:
        groups = [group for group in groups if next(group, "end") != "end"]
    for which in range(2):
        for g in range(KVH):
            halo_x(which, g).wait_send()
            halo_y(which, g).wait_send()
            back_y(which, g).wait_send()
            back_x(which, g).wait_send()


def fused(lengths, q_rows, k_rows, v_rows, do_rows, x_rows):
    scratch = [
        pltpu.VMEM((KVH, 768, HD), BF),
        pltpu.VMEM((KVH, 768, HD), BF),
        pltpu.VMEM((2, SPAN, GROUP * HALF), F32),
        pltpu.VMEM((KVH, 2, SPAN, GROUP * HALF), BF),
        pltpu.VMEM((768, HD), F32),
        pltpu.VMEM((2, KVH, 256, HD), BF),
        pltpu.VMEM((2, KVH, 256, HD), BF),
        pltpu.VMEM((2, KVH, 256, HD), BF),
        pltpu.VMEM((2, KVH, 256, HD), BF),
        pltpu.VMEM((2, KVH, 256, HD), F32),
        pltpu.VMEM((256, 2048), BF),
        pltpu.VMEM((512, 1024), BF),
        pltpu.VMEM((2, 8, 4, 32, 512), BF),
        pltpu.SemaphoreType.DMA((2, 8, KVH)),
        pltpu.SemaphoreType.DMA((2, 6)),
    ]
    for _, width, first in GROUPS:
        scratch += group_scratch(width, first)
    return pl.pallas_call(
        fused_kernel,
        out_shape=(
            jax.ShapeDtypeStruct((256, 4096), BF),
            jax.ShapeDtypeStruct((256, 1024), BF),
            jax.ShapeDtypeStruct((256, 1024), BF),
            jax.ShapeDtypeStruct((16, 1024), F32),
        ),
        in_specs=[pl.BlockSpec(memory_space=pltpu.VMEM)] * 6,
        out_specs=[pl.BlockSpec(memory_space=pltpu.VMEM)] * 4,
        scratch_shapes=scratch,
        compiler_params=pltpu.CompilerParams(
            collective_id=1, has_side_effects=True, vmem_limit_bytes=60 * 2**20
        ),
        cost_estimate=pl.CostEstimate(flops=10**10, bytes_accessed=12 * 2**20, transcendentals=6 * 10**6),
    )(lengths, q_rows, k_rows, v_rows, do_rows, x_rows)


def local(queries, keys, values, out_grad, layer_input, doc_lengths):
    outs = fused(doc_lengths, queries[0], keys[0], values[0], out_grad[0], layer_input[0])
    return (outs[0][None], outs[1][None], outs[2][None], outs[3])


def solution(mesh):
    placed = (
        P("dp", "ctx", None),
        P("dp", "ctx", None),
        P("dp", "ctx", None),
        P("dp", "ctx", None),
        P("dp", "ctx", None),
        P("dp", None),
    )
    return jax.shard_map(
        local,
        mesh=mesh,
        in_specs=placed,
        out_specs=(
            P("dp", "ctx", None),
            P("dp", "ctx", None),
            P("dp", "ctx", None),
            P(("dp", "ctx"), None),
        ),
        check_vma=False,
    )
```

```python
import jax
import jax.numpy as jnp
from jax import lax
from jax.experimental import pallas as pl
from jax.experimental.pallas import tpu as pltpu
from jax.sharding import PartitionSpec as P

KVH = 8
HD = 128
GROUP = 4
LEAD = 3
LAG = 3
RS_AT = (0, 3, 6, 9, 12)
SWAP_TICK = 4
VLATE = (5, 6, 6, 7, 7, 8, 8, 9)
P2_FROM = 15
KINDS = "xyxyxyxy"
RS_LATE = 1
VMEM_MB = 48
BF = jnp.bfloat16
F32 = jnp.float32


MESH = pl.DeviceIdType.MESH
GROUPS = tuple((g * 128, 128, kind) for g, kind in enumerate(KINDS))
SIZES = {"core": 2, "y": 4, "x": 4, "z": 8}


def place():
    dp, ctx = lax.axis_index("dp"), lax.axis_index("ctx")
    return {
        "core": lax.rem(dp, 2),
        "y": lax.rem(ctx, 2) * 2 + dp // 2,
        "x": lax.rem(ctx // 2, 4),
        "z": ctx // 8,
    }


def member(here, axis, step):
    return lax.rem(here[axis] + (step + SIZES[axis]), SIZES[axis])


def at(here, axis, step):
    spot = dict(here)
    spot[axis] = member(here, axis, step)
    dp = lax.rem(spot["y"], 2) * 2 + spot["core"]
    ctx = spot["z"] * 8 + spot["x"] * 2 + spot["y"] // 2
    return (dp, ctx)


def push(src, dst, sems, slot, target):
    copy = pltpu.make_async_remote_copy(
        src_ref=src,
        dst_ref=dst,
        send_sem=sems.at[0, slot],
        recv_sem=sems.at[1, slot],
        device_id=target,
        device_id_type=MESH,
    )
    copy.start()
    return copy


def ring(here, axis, term, keep, out, inn, sems):
    half = SIZES[axis] // 2
    count = out.shape[2]
    mid = count // 2
    ends = (at(here, axis, 1), at(here, axis, -1))
    far = term(member(here, axis, half)).astype(BF)
    copies = [[], []]
    for way in range(2):
        part = pl.ds(way * mid, mid)
        out[way, 0, part] = far[way * mid : (way + 1) * mid]
        copies[way].append(push(out.at[way, 0, part], inn.at[way, 0, part], sems, way, ends[way]))
    yield
    for step in range(1, half):
        for way in range(2):
            mine = term(member(here, axis, (half - step) * (1 - 2 * way)))
            copies[way][-1].wait_recv()
            if step == 1:
                got, rest = slice(way * mid, (way + 1) * mid), slice((1 - way) * mid, (2 - way) * mid)
                out[way, 1, got] = (mine[got] + inn[way, 0, got].astype(F32)).astype(BF)
                out[way, 1, rest] = mine[rest].astype(BF)
            else:
                out[way, step] = (mine + inn[way, step - 1].astype(F32)).astype(BF)
            copies[way].append(push(out.at[way, step], inn.at[way, step], sems, 2 * step + way, ends[way]))
        yield
    mine = term(here[axis])
    copies[0][-1].wait_recv()
    copies[1][-1].wait_recv()
    keep(mine + inn[0, half - 1].astype(F32) + inn[1, half - 1].astype(F32))
    for copy in copies[0] + copies[1]:
        copy.wait_send()


def direct(here, axis, term, keep, out, inn, sems, base):
    size = SIZES[axis]
    copies = []
    for step in sorted(range(1, size), key=lambda step: -min(step, size - step)):
        out[step - 1] = term(member(here, axis, step)).astype(BF)
        copies.append(push(out.at[step - 1], inn.at[step - 1], sems, base + step - 1, at(here, axis, step)))
    yield
    value = term(here[axis])
    for copy in copies:
        copy.wait_recv()
    for step in range(size - 1):
        value = value + inn[step].astype(F32)
    keep(value)
    for copy in copies:
        copy.wait_send()


def scatter_group(here, xt, dvg, out_ref, c0, width, first, big_out, big_in, small_out, small_in, mid_sum, low_sum, last_out, last_in, sems):
    def pieces(axis, index):
        if axis == "x":
            return xt[:, :, index].reshape(512, 512)
        return xt[lax.rem(index, 2), :, :, index // 2].reshape(512, 512)

    def product(index):
        return jnp.dot(pieces(first, index), dvg[:, c0 : c0 + width], preferred_element_type=F32)

    def middle(index):
        part = mid_sum[:, index] if first == "y" else mid_sum[lax.rem(index, 2), :, index // 2]
        return part.reshape(128, width)

    def low(index):
        return low_sum[index]

    def keep_mid(value):
        mid_sum[...] = value.reshape(mid_sum.shape)

    def keep_low(value):
        low_sum[...] = value.reshape(low_sum.shape)

    def keep_out(value):
        out_ref[:, c0 : c0 + width] = value

    yield from ring(here, first, product, keep_mid, big_out, big_in, sems)
    yield from direct(here, "x" if first == "y" else "y", middle, keep_low, small_out, small_in, sems, 4)
    yield from direct(here, "z", low, keep_out, last_out, last_in, sems, 7)


def group_scratch(width, first):
    mid = (8, 4, 16) if first == "y" else (2, 8, 2, 16)
    return [
        pltpu.VMEM((2, 2, 512, width), BF),
        pltpu.VMEM((2, 2, 512, width), BF),
        pltpu.VMEM((3, 128, width), BF),
        pltpu.VMEM((3, 128, width), BF),
        pltpu.VMEM((*mid, width), F32),
        pltpu.VMEM((8, 16, width), F32),
        pltpu.VMEM((7, 16, width), BF),
        pltpu.VMEM((7, 16, width), BF),
        pltpu.SemaphoreType.DMA((2, 14)),
    ]


SPAN = 640
HALF = 128
SCALE = HD ** (-0.5)


def dot_nt(left, right):
    return lax.dot_general(left, right, (((1,), (1,)), ((), ())), preferred_element_type=F32)


def dot_nn(left, right):
    return jnp.dot(left, right, preferred_element_type=F32)


def head_columns(head, count=1):
    return pl.ds(pl.multiple_of(head * HD, HD), count * HD)


def stacked(ref, g, half):
    rows = pl.ds(half * HALF, HALF)
    return jnp.concatenate([ref[rows, head_columns(g * GROUP + e)] for e in range(GROUP)], axis=0)


def fill_bias(lengths_ref, slab, bias):
    row = lax.broadcasted_iota(jnp.int32, (64, 64), 0)
    col = lax.broadcasted_iota(jnp.int32, (64, 64), 1)
    sizes = jnp.broadcast_to(lengths_ref[...], (64, 64))
    starts = jnp.sum(jnp.where(col < row, sizes, 0), axis=1, keepdims=True)
    for half in range(2):
        base = slab * 256 + half * HALF
        query = base + lax.broadcasted_iota(jnp.int32, (64, HALF), 1)
        first = jnp.max(jnp.where(starts <= query, starts, 0), axis=0, keepdims=True)
        key = base - 512 + lax.broadcasted_iota(jnp.int32, (SPAN, HALF), 0)
        query = base + lax.broadcasted_iota(jnp.int32, (SPAN, HALF), 1)
        value = jnp.where((key <= query) & (key >= first), 0.0, -1e30)
        for e in range(GROUP):
            bias[half, :, e * HALF : (e + 1) * HALF] = value


def probs_step(g, q_ref, do_ref, kwin, bias, pbuf, dvwin):
    for half in range(2):
        rows = pl.ds(half * HALF, SPAN)
        scores = dot_nt(kwin[g, rows], stacked(q_ref, g, half)) * (SCALE * 1.4426950408889634) + bias[half]
        top = jnp.max(scores, axis=0, keepdims=True)
        weights = jnp.exp2(scores - top)
        probs = (weights * (1.0 / jnp.sum(weights, axis=0, keepdims=True))).astype(BF)
        pbuf[g, half] = probs
        term = dot_nn(probs, stacked(do_ref, g, half))
        if half == 0:
            dvwin[0:SPAN] = term
            dvwin[SPAN:768] = jnp.zeros((HALF, HD), F32)
        else:
            dvwin[rows] += term


def grads_step(g, q_ref, do_ref, kwin, vwin, pbuf, dkwin, dq_ref):
    turned = kwin[g].T
    for half in range(2):
        rows = pl.ds(half * HALF, SPAN)
        probs = pbuf[g, half].astype(F32)
        dprobs = dot_nt(vwin[g, rows], stacked(do_ref, g, half))
        delta = jnp.sum(probs * dprobs, axis=0, keepdims=True)
        dscores = (probs * (dprobs - delta)).astype(BF)
        term = dot_nn(dscores, stacked(q_ref, g, half))
        if half == 0:
            dkwin[0:SPAN] = term
            dkwin[SPAN:768] = jnp.zeros((HALF, HD), F32)
        else:
            dkwin[rows] += term
        dq = dot_nn(turned[:, half * HALF : half * HALF + SPAN], dscores) * SCALE
        for e in range(GROUP):
            dq_ref[pl.ds(half * HALF, HALF), head_columns(g * GROUP + e)] = dq[:, e * HALF : (e + 1) * HALF].T.astype(BF)


def fused_kernel(lengths_hbm, q_hbm, k_hbm, v_hbm, do_hbm, x_hbm, dq_ref, dk_ref, dv_ref, dw_ref,
                 lengths_ref, q_ref, do_ref, x_ref, kwin, vwin, bias, pbuf, window, out1, in1, out2, in2, final,
                 xrecv, dvg, xt, load_sems, slab_sems, halo_sems, pair_sems, *scratch):
    here = place()
    dp, ctx = lax.axis_index("dp"), lax.axis_index("ctx")
    odd = lax.rem(ctx, 2)
    twin = (dp, ctx + 1 - 2 * odd)
    ahead, behind = (dp, lax.rem(ctx + 2, 64)), (dp, lax.rem(ctx + 62, 64))
    partner = at(here, "core", 1)
    relay = pl.multiple_of(512 * (1 - odd), 256)

    def link(src, dst, kind, g, target):
        return pltpu.make_async_remote_copy(
            src_ref=src, dst_ref=dst, send_sem=halo_sems.at[0, kind, g], recv_sem=halo_sems.at[1, kind, g],
            device_id=target, device_id_type=MESH)

    def halo_x(which, g):
        win = (kwin, vwin)[which]
        return link(win.at[g, pl.ds(512, 256)], win.at[g, pl.ds(0, 256)], 2 * which, g, ahead)

    def halo_y(which, g):
        win = (kwin, vwin)[which]
        return link(win.at[g, pl.ds(relay, 256)], win.at[g, pl.ds(256, 256)], 2 * which + 1, g, twin)

    def back_y(which, g):
        return link(out1.at[which, g], in1.at[which, g], 4 + 2 * which, g, twin)

    def back_x(which, g):
        return link(out2.at[which, g], in2.at[which, g], 5 + 2 * which, g, behind)

    def relayed(which, g):
        @pl.when(odd == 1)
        def _():
            halo_x(which, g).wait_recv()
            halo_y(which, g).start()

    def own_first(which, g):
        @pl.when(odd == 0)
        def _():
            halo_y(which, g).start()

    def arrived(which, g):
        halo_y(which, g).wait_recv()

        @pl.when(odd == 0)
        def _():
            halo_x(which, g).wait_recv()

    def give_near(which, g):
        out1[which, g] = window[256:512].astype(BF)
        back_y(which, g).start()
        final[which, g] = window[512:768]
        out2[which, g] = window[0:256].astype(BF)

    def give_far(which, g):
        back_y(which, g).wait_recv()
        got = in1[which, g].astype(F32)
        out2[which, g] = (out2[which, g].astype(F32) + jnp.where(odd == 1, got, 0.0)).astype(BF)
        back_x(which, g).start()
        final[which, g] += jnp.where(odd == 1, 0.0, got)

    def finish(which, g):
        back_x(which, g).wait_recv()
        total = final[which, g] + in2[which, g].astype(F32)
        if which == 0:
            dk_ref[:, head_columns(g)] = (total * SCALE).astype(BF)
        else:
            rounded = total.astype(BF)
            dv_ref[:, head_columns(g)] = rounded
            dvg[0:256, head_columns(g)] = rounded

    shares = {}

    def share(g):
        columns = pl.ds(g * HD, HD)
        shares[g] = push(dvg.at[pl.ds(0, 256), columns], dvg.at[pl.ds(256, 256), columns], pair_sems, 2 + g, partner)

    loads = [
        pltpu.make_async_copy(src, dst, load_sems.at[i])
        for i, (src, dst) in enumerate(((lengths_hbm, lengths_ref), (x_hbm, x_ref), (q_hbm, q_ref), (do_hbm, do_ref)))
    ]
    slabs = [
        [
            pltpu.make_async_copy(src.at[:, pl.ds(g * HD, HD)], win.at[g, pl.ds(512, 256)], slab_sems.at[which, g])
            for g in range(KVH)
        ]
        for which, (src, win) in enumerate(((k_hbm, kwin), (v_hbm, vwin)))
    ]
    for slab in slabs[0]:
        slab.start()
    for load in loads:
        load.start()
    for slab in slabs[1]:
        slab.start()
    greeted = [partner, ahead, behind]
    greeted += [at(here, axis, step) for axis in "xyz" for step in range(1, SIZES[axis])]
    barrier = pltpu.get_barrier_semaphore()
    for target in greeted:
        pl.semaphore_signal(barrier, inc=1, device_id=target, device_id_type=MESH)
    pl.semaphore_wait(barrier, len(greeted))
    for g in range(KVH):
        slabs[0][g].wait()
        halo_x(0, g).start()
        own_first(0, g)
    mine, other = here["core"] * 1024, (1 - here["core"]) * 1024
    loads[0].wait()
    loads[1].wait()
    swaps = []
    for part in range(2):
        columns = pl.ds(pl.multiple_of(part * 2048 + other, 128), 1024)
        swaps.append(push(x_ref.at[:, columns], xrecv.at[:, pl.ds(part * 1024, 1024)], pair_sems, part, partner))
    for slab in slabs[1]:
        slab.wait()
    fill_bias(lengths_ref, ctx, bias)
    for g in range(LEAD):
        relayed(0, g)
    for part in range(2):
        def own(z, carry):
            columns = pl.ds(pl.multiple_of(part * 2048 + mine + z * 128, 128), 128)
            xt[part, z, :, :, :, 0:256] = x_ref[:, columns].T.reshape(4, 2, 16, 256)
            return carry
        lax.fori_loop(0, 8, own, 0)
    loads[2].wait()
    loads[3].wait()

    groups = {}
    for tick in range(max(P2_FROM + KVH + 2 * LAG, 2 * LAG + KVH + RS_LATE + RS_AT[-1])):
        if tick < KVH:
            halo_x(1, tick).start()
        for g in range(KVH):
            if VLATE[g] == tick:
                own_first(1, g)
                relayed(1, g)
        if tick + LEAD < KVH:
            relayed(0, tick + LEAD)
        if tick < KVH:
            arrived(0, tick)
            probs_step(tick, q_ref, do_ref, kwin, bias, pbuf, window)
            give_near(1, tick)
        elif P2_FROM <= tick < P2_FROM + KVH:
            arrived(1, tick - P2_FROM)
            grads_step(tick - P2_FROM, q_ref, do_ref, kwin, vwin, pbuf, window, dq_ref)
            give_near(0, tick - P2_FROM)
        if tick == SWAP_TICK:
            swaps[0].wait()
            swaps[1].wait()
            for part in range(2):
                def got(z, carry):
                    columns = pl.ds(pl.multiple_of(part * 1024 + z * 128, 128), 128)
                    xt[part, z, :, :, :, 256:512] = xrecv[:, columns].T.reshape(4, 2, 16, 256)
                    return carry
                lax.fori_loop(0, 8, got, 0)
        for which in (1, 0):
            g = tick - (1 - which) * P2_FROM - LAG
            if 0 <= g < KVH:
                give_far(which, g)
            if 0 <= g - LAG < KVH:
                finish(which, g - LAG)
                if which == 1:
                    share(g - LAG)
        for i in range(KVH):
            since = tick - (2 * LAG + i + RS_LATE)
            if since == 0:
                shares[i].wait()
                c0, width, first = GROUPS[i]
                groups[i] = scatter_group(here, xt, dvg, dw_ref, c0, width, first, *scratch[i * 9 : (i + 1) * 9])
            if since in RS_AT and i in groups:
                next(groups[i], None)
    for which in range(2):
        for g in range(KVH):
            halo_x(which, g).wait_send()
            halo_y(which, g).wait_send()
            back_y(which, g).wait_send()
            back_x(which, g).wait_send()


def fused(lengths, q_rows, k_rows, v_rows, do_rows, x_rows):
    scratch = [
        pltpu.VMEM((1, 64), jnp.int32),
        pltpu.VMEM((256, 4096), BF),
        pltpu.VMEM((256, 4096), BF),
        pltpu.VMEM((256, 4096), BF),
        pltpu.VMEM((KVH, 768, HD), BF),
        pltpu.VMEM((KVH, 768, HD), BF),
        pltpu.VMEM((2, SPAN, GROUP * HALF), F32),
        pltpu.VMEM((KVH, 2, SPAN, GROUP * HALF), BF),
        pltpu.VMEM((768, HD), F32),
        pltpu.VMEM((2, KVH, 256, HD), BF),
        pltpu.VMEM((2, KVH, 256, HD), BF),
        pltpu.VMEM((2, KVH, 256, HD), BF),
        pltpu.VMEM((2, KVH, 256, HD), BF),
        pltpu.VMEM((2, KVH, 256, HD), F32),
        pltpu.VMEM((256, 2048), BF),
        pltpu.VMEM((512, 1024), BF),
        pltpu.VMEM((2, 8, 4, 2, 16, 512), BF),
        pltpu.SemaphoreType.DMA((4,)),
        pltpu.SemaphoreType.DMA((2, KVH)),
        pltpu.SemaphoreType.DMA((2, 8, KVH)),
        pltpu.SemaphoreType.DMA((2, 10)),
    ]
    for _, width, first in GROUPS:
        scratch += group_scratch(width, first)
    vmem, hbm = pl.BlockSpec(memory_space=pltpu.VMEM), pl.BlockSpec(memory_space=pltpu.HBM)
    return pl.pallas_call(
        fused_kernel,
        out_shape=(
            jax.ShapeDtypeStruct((256, 4096), BF),
            jax.ShapeDtypeStruct((256, 1024), BF),
            jax.ShapeDtypeStruct((256, 1024), BF),
            jax.ShapeDtypeStruct((16, 1024), F32),
        ),
        in_specs=[hbm] * 6,
        out_specs=[vmem] * 4,
        scratch_shapes=scratch,
        compiler_params=pltpu.CompilerParams(
            collective_id=1, has_side_effects=True, vmem_limit_bytes=VMEM_MB * 2**20
        ),
        cost_estimate=pl.CostEstimate(flops=10**10, bytes_accessed=12 * 2**20, transcendentals=6 * 10**6),
    )(lengths, q_rows, k_rows, v_rows, do_rows, x_rows)


def store_kernel(*refs):
    copies = [pltpu.make_async_copy(refs[i], refs[4 + i], refs[8].at[i]) for i in range(4)]
    for copy in copies:
        copy.start()
    for copy in copies:
        copy.wait()


def store(outs):
    return pl.pallas_call(
        store_kernel,
        out_shape=tuple(jax.ShapeDtypeStruct(out.shape, out.dtype) for out in outs),
        in_specs=[pl.BlockSpec(memory_space=pl.ANY)] * 4,
        out_specs=[pl.BlockSpec(memory_space=pltpu.HBM)] * 4,
        scratch_shapes=[pltpu.SemaphoreType.DMA((4,))],
        compiler_params=pltpu.CompilerParams(vmem_limit_bytes=2**20),
    )(*outs)


def local(queries, keys, values, out_grad, layer_input, doc_lengths):
    rows = (doc_lengths, queries[0], keys[0], values[0], out_grad[0], layer_input[0])
    outs = store(fused(*[pltpu.with_memory_space_constraint(part, pltpu.HBM) for part in rows]))
    return (outs[0][None], outs[1][None], outs[2][None], outs[3])


def solution(mesh):
    placed = (
        P("dp", "ctx", None),
        P("dp", "ctx", None),
        P("dp", "ctx", None),
        P("dp", "ctx", None),
        P("dp", "ctx", None),
        P("dp", None),
    )
    return jax.shard_map(
        local,
        mesh=mesh,
        in_specs=placed,
        out_specs=(
            P("dp", "ctx", None),
            P("dp", "ctx", None),
            P("dp", "ctx", None),
            P(("dp", "ctx"), None),
        ),
        check_vma=False,
    )
```

```python
import jax
import jax.numpy as jnp
from jax import lax
from jax.experimental import pallas as pl
from jax.experimental.pallas import tpu as pltpu
from jax.sharding import PartitionSpec as P

KVH = 8
HD = 128
GROUP = 4
LEAD = 3
LAG = 3
RS_AT = {"x": (0, 3, 6, 9, 12), "z": (0, 2, 5, 8, 11, 14, 17)}
SWAP_TICK = 4
VLATE = (5, 6, 6, 7, 7, 8, 8, 9)
P2_FROM = 15
KINDS = "zzxzxzxx"
RS_LATE = 1
VMEM_MB = 48
BF = jnp.bfloat16
F32 = jnp.float32


MESH = pl.DeviceIdType.MESH
GROUPS = tuple((g * 128, 128, kind) for g, kind in enumerate(KINDS))
SIZES = {"core": 2, "y": 4, "x": 4, "z": 8}


def place():
    dp, ctx = lax.axis_index("dp"), lax.axis_index("ctx")
    return {
        "core": lax.rem(dp, 2),
        "y": lax.rem(ctx, 2) * 2 + dp // 2,
        "x": lax.rem(ctx // 2, 4),
        "z": ctx // 8,
    }


def member(here, axis, step):
    return lax.rem(here[axis] + (step + SIZES[axis]), SIZES[axis])


def at(here, axis, step):
    spot = dict(here)
    spot[axis] = member(here, axis, step)
    dp = lax.rem(spot["y"], 2) * 2 + spot["core"]
    ctx = spot["z"] * 8 + spot["x"] * 2 + spot["y"] // 2
    return (dp, ctx)


def push(src, dst, sems, slot, target):
    copy = pltpu.make_async_remote_copy(
        src_ref=src,
        dst_ref=dst,
        send_sem=sems.at[0, slot],
        recv_sem=sems.at[1, slot],
        device_id=target,
        device_id_type=MESH,
    )
    copy.start()
    return copy


def ring(here, axis, term, keep, out, inn, sems):
    half = SIZES[axis] // 2
    count = out.shape[2]
    mid = count // 2
    ends = (at(here, axis, 1), at(here, axis, -1))
    far = term(member(here, axis, half)).astype(BF)
    copies = [[], []]
    for way in range(2):
        part = pl.ds(way * mid, mid)
        out[way, 0, part] = far[way * mid : (way + 1) * mid]
        copies[way].append(push(out.at[way, 0, part], inn.at[way, 0, part], sems, way, ends[way]))
    yield
    for step in range(1, half):
        for way in range(2):
            mine = term(member(here, axis, (half - step) * (1 - 2 * way)))
            copies[way][-1].wait_recv()
            if step == 1:
                got, rest = slice(way * mid, (way + 1) * mid), slice((1 - way) * mid, (2 - way) * mid)
                out[way, 1, got] = (mine[got] + inn[way, 0, got].astype(F32)).astype(BF)
                out[way, 1, rest] = mine[rest].astype(BF)
            else:
                out[way, step] = (mine + inn[way, step - 1].astype(F32)).astype(BF)
            copies[way].append(push(out.at[way, step], inn.at[way, step], sems, 2 * step + way, ends[way]))
        yield
    mine = term(here[axis])
    copies[0][-1].wait_recv()
    copies[1][-1].wait_recv()
    keep(mine + inn[0, half - 1].astype(F32) + inn[1, half - 1].astype(F32))
    for copy in copies[0] + copies[1]:
        copy.wait_send()


def direct(here, axis, term, keep, out, inn, sems, base):
    size = SIZES[axis]
    copies = []
    for step in sorted(range(1, size), key=lambda step: -min(step, size - step)):
        out[step - 1] = term(member(here, axis, step)).astype(BF)
        copies.append(push(out.at[step - 1], inn.at[step - 1], sems, base + step - 1, at(here, axis, step)))
    yield
    value = term(here[axis])
    for copy in copies:
        copy.wait_recv()
    for step in range(size - 1):
        value = value + inn[step].astype(F32)
    keep(value)
    for copy in copies:
        copy.wait_send()


def scatter_group(here, xt, dvg, out_ref, c0, width, first, big_out, big_in, small_out, small_in, mid_sum, low_sum, last_out, last_in, sems):
    def pieces(index):
        return xt[:, index].reshape(256, 512) if first == "z" else xt[:, :, index].reshape(512, 512)

    def product(index):
        return jnp.dot(pieces(index), dvg[:, c0 : c0 + width], preferred_element_type=F32)

    def middle(index):
        if first == "z":
            return mid_sum[:, index].reshape(64, width)
        return mid_sum[lax.rem(index, 2), :, index // 2].reshape(128, width)

    def low(index):
        return low_sum[lax.rem(index, 2), index // 2] if first == "z" else low_sum[index]

    def keep_mid(value):
        mid_sum[...] = value.reshape(mid_sum.shape)

    def keep_low(value):
        low_sum[...] = value.reshape(low_sum.shape)

    def keep_out(value):
        out_ref[:, c0 : c0 + width] = value

    yield from ring(here, first, product, keep_mid, big_out, big_in, sems)
    yield from direct(here, "x" if first == "z" else "y", middle, keep_low, small_out, small_in, sems, 8)
    yield from direct(here, "y" if first == "z" else "z", low, keep_out, last_out, last_in, sems, 11)


def group_scratch(width, first):
    if first == "z":
        big, small, last, mid, low = (4, 256), 64, 3, (2, 4, 32), (2, 2, 16)
    else:
        big, small, last, mid, low = (2, 512), 128, 7, (2, 8, 2, 16), (8, 16)
    return [
        pltpu.VMEM((2, *big, width), BF),
        pltpu.VMEM((2, *big, width), BF),
        pltpu.VMEM((3, small, width), BF),
        pltpu.VMEM((3, small, width), BF),
        pltpu.VMEM((*mid, width), F32),
        pltpu.VMEM((*low, width), F32),
        pltpu.VMEM((last, 16, width), BF),
        pltpu.VMEM((last, 16, width), BF),
        pltpu.SemaphoreType.DMA((2, 18)),
    ]


SPAN = 640
HALF = 128
SCALE = HD ** (-0.5)


def dot_nt(left, right):
    return lax.dot_general(left, right, (((1,), (1,)), ((), ())), preferred_element_type=F32)


def dot_nn(left, right):
    return jnp.dot(left, right, preferred_element_type=F32)


def head_columns(head, count=1):
    return pl.ds(pl.multiple_of(head * HD, HD), count * HD)


def stacked(ref, g, half):
    rows = pl.ds(half * HALF, HALF)
    return jnp.concatenate([ref[rows, head_columns(g * GROUP + e)] for e in range(GROUP)], axis=0)


def fill_bias(lengths_ref, slab, bias):
    row = lax.broadcasted_iota(jnp.int32, (64, 64), 0)
    col = lax.broadcasted_iota(jnp.int32, (64, 64), 1)
    sizes = jnp.broadcast_to(lengths_ref[...], (64, 64))
    starts = jnp.sum(jnp.where(col < row, sizes, 0), axis=1, keepdims=True)
    for half in range(2):
        base = slab * 256 + half * HALF
        query = base + lax.broadcasted_iota(jnp.int32, (64, HALF), 1)
        first = jnp.max(jnp.where(starts <= query, starts, 0), axis=0, keepdims=True)
        key = base - 512 + lax.broadcasted_iota(jnp.int32, (SPAN, HALF), 0)
        query = base + lax.broadcasted_iota(jnp.int32, (SPAN, HALF), 1)
        value = jnp.where((key <= query) & (key >= first), 0.0, -1e30)
        for e in range(GROUP):
            bias[half, :, e * HALF : (e + 1) * HALF] = value


def probs_step(g, q_ref, do_ref, kwin, bias, pbuf, dvwin):
    for half in range(2):
        rows = pl.ds(half * HALF, SPAN)
        scores = dot_nt(kwin[g, rows], stacked(q_ref, g, half)) * (SCALE * 1.4426950408889634) + bias[half]
        top = jnp.max(scores, axis=0, keepdims=True)
        weights = jnp.exp2(scores - top)
        probs = (weights * (1.0 / jnp.sum(weights, axis=0, keepdims=True))).astype(BF)
        pbuf[g, half] = probs
        term = dot_nn(probs, stacked(do_ref, g, half))
        if half == 0:
            dvwin[0:SPAN] = term
            dvwin[SPAN:768] = jnp.zeros((HALF, HD), F32)
        else:
            dvwin[rows] += term


def grads_step(g, q_ref, do_ref, kwin, vwin, pbuf, dkwin, dq_ref):
    turned = kwin[g].T
    for half in range(2):
        rows = pl.ds(half * HALF, SPAN)
        probs = pbuf[g, half].astype(F32)
        dprobs = dot_nt(vwin[g, rows], stacked(do_ref, g, half))
        delta = jnp.sum(probs * dprobs, axis=0, keepdims=True)
        dscores = (probs * (dprobs - delta)).astype(BF)
        term = dot_nn(dscores, stacked(q_ref, g, half))
        if half == 0:
            dkwin[0:SPAN] = term
            dkwin[SPAN:768] = jnp.zeros((HALF, HD), F32)
        else:
            dkwin[rows] += term
        dq = dot_nn(turned[:, half * HALF : half * HALF + SPAN], dscores) * SCALE
        for e in range(GROUP):
            dq_ref[pl.ds(half * HALF, HALF), head_columns(g * GROUP + e)] = dq[:, e * HALF : (e + 1) * HALF].T.astype(BF)


def fused_kernel(lengths_hbm, q_hbm, k_hbm, v_hbm, do_hbm, x_hbm, dq_ref, dk_ref, dv_ref, dw_ref,
                 lengths_ref, q_ref, do_ref, x_ref, kwin, vwin, bias, pbuf, window, out1, in1, out2, in2, final,
                 xrecv, dvg, xt, load_sems, slab_sems, halo_sems, pair_sems, *scratch):
    here = place()
    dp, ctx = lax.axis_index("dp"), lax.axis_index("ctx")
    odd = lax.rem(ctx, 2)
    twin = (dp, ctx + 1 - 2 * odd)
    ahead, behind = (dp, lax.rem(ctx + 2, 64)), (dp, lax.rem(ctx + 62, 64))
    partner = at(here, "core", 1)
    relay = pl.multiple_of(512 * (1 - odd), 256)

    def link(src, dst, kind, g, target):
        return pltpu.make_async_remote_copy(
            src_ref=src, dst_ref=dst, send_sem=halo_sems.at[0, kind, g], recv_sem=halo_sems.at[1, kind, g],
            device_id=target, device_id_type=MESH)

    def halo_x(which, g):
        win = (kwin, vwin)[which]
        return link(win.at[g, pl.ds(512, 256)], win.at[g, pl.ds(0, 256)], 2 * which, g, ahead)

    def halo_y(which, g):
        win = (kwin, vwin)[which]
        return link(win.at[g, pl.ds(relay, 256)], win.at[g, pl.ds(256, 256)], 2 * which + 1, g, twin)

    def back_y(which, g):
        return link(out1.at[which, g], in1.at[which, g], 4 + 2 * which, g, twin)

    def back_x(which, g):
        return link(out2.at[which, g], in2.at[which, g], 5 + 2 * which, g, behind)

    def relayed(which, g):
        @pl.when(odd == 1)
        def _():
            halo_x(which, g).wait_recv()
            halo_y(which, g).start()

    def own_first(which, g):
        @pl.when(odd == 0)
        def _():
            halo_y(which, g).start()

    def arrived(which, g):
        halo_y(which, g).wait_recv()

        @pl.when(odd == 0)
        def _():
            halo_x(which, g).wait_recv()

    def give_near(which, g):
        out1[which, g] = window[256:512].astype(BF)
        back_y(which, g).start()
        final[which, g] = window[512:768]
        out2[which, g] = window[0:256].astype(BF)

    def give_far(which, g):
        back_y(which, g).wait_recv()
        got = in1[which, g].astype(F32)
        out2[which, g] = (out2[which, g].astype(F32) + jnp.where(odd == 1, got, 0.0)).astype(BF)
        back_x(which, g).start()
        final[which, g] += jnp.where(odd == 1, 0.0, got)

    def finish(which, g):
        back_x(which, g).wait_recv()
        total = final[which, g] + in2[which, g].astype(F32)
        if which == 0:
            dk_ref[:, head_columns(g)] = (total * SCALE).astype(BF)
        else:
            rounded = total.astype(BF)
            dv_ref[:, head_columns(g)] = rounded
            dvg[0:256, head_columns(g)] = rounded

    shares = {}

    def share(g):
        columns = pl.ds(g * HD, HD)
        shares[g] = push(dvg.at[pl.ds(0, 256), columns], dvg.at[pl.ds(256, 256), columns], pair_sems, 2 + g, partner)

    loads = [
        pltpu.make_async_copy(src, dst, load_sems.at[i])
        for i, (src, dst) in enumerate(((lengths_hbm, lengths_ref), (x_hbm, x_ref), (q_hbm, q_ref), (do_hbm, do_ref)))
    ]
    slabs = [
        [
            pltpu.make_async_copy(src.at[:, pl.ds(g * HD, HD)], win.at[g, pl.ds(512, 256)], slab_sems.at[which, g])
            for g in range(KVH)
        ]
        for which, (src, win) in enumerate(((k_hbm, kwin), (v_hbm, vwin)))
    ]
    for slab in slabs[0]:
        slab.start()
    for load in loads:
        load.start()
    for slab in slabs[1]:
        slab.start()
    greeted = [partner, ahead, behind]
    greeted += [at(here, axis, step) for axis in "xyz" for step in range(1, SIZES[axis])]
    barrier = pltpu.get_barrier_semaphore()
    for target in greeted:
        pl.semaphore_signal(barrier, inc=1, device_id=target, device_id_type=MESH)
    pl.semaphore_wait(barrier, len(greeted))
    for g in range(KVH):
        slabs[0][g].wait()
        halo_x(0, g).start()
        own_first(0, g)
    mine, other = here["core"] * 1024, (1 - here["core"]) * 1024
    loads[0].wait()
    loads[1].wait()
    swaps = []
    for part in range(2):
        columns = pl.ds(pl.multiple_of(part * 2048 + other, 128), 1024)
        swaps.append(push(x_ref.at[:, columns], xrecv.at[:, pl.ds(part * 1024, 1024)], pair_sems, part, partner))
    for slab in slabs[1]:
        slab.wait()
    fill_bias(lengths_ref, ctx, bias)
    for g in range(LEAD):
        relayed(0, g)
    for part in range(2):
        def own(z, carry):
            columns = pl.ds(pl.multiple_of(part * 2048 + mine + z * 128, 128), 128)
            xt[part, z, :, :, :, 0:256] = x_ref[:, columns].T.reshape(4, 2, 16, 256)
            return carry
        lax.fori_loop(0, 8, own, 0)
    loads[2].wait()
    loads[3].wait()

    groups = {}
    for tick in range(max(P2_FROM + KVH + 2 * LAG, 2 * LAG + KVH + RS_LATE + 17)):
        if tick < KVH:
            halo_x(1, tick).start()
        for g in range(KVH):
            if VLATE[g] == tick:
                own_first(1, g)
                relayed(1, g)
        if tick + LEAD < KVH:
            relayed(0, tick + LEAD)
        if tick < KVH:
            arrived(0, tick)
            probs_step(tick, q_ref, do_ref, kwin, bias, pbuf, window)
            give_near(1, tick)
        elif P2_FROM <= tick < P2_FROM + KVH:
            arrived(1, tick - P2_FROM)
            grads_step(tick - P2_FROM, q_ref, do_ref, kwin, vwin, pbuf, window, dq_ref)
            give_near(0, tick - P2_FROM)
        if tick == SWAP_TICK:
            swaps[0].wait()
            swaps[1].wait()
            for part in range(2):
                def got(z, carry):
                    columns = pl.ds(pl.multiple_of(part * 1024 + z * 128, 128), 128)
                    xt[part, z, :, :, :, 256:512] = xrecv[:, columns].T.reshape(4, 2, 16, 256)
                    return carry
                lax.fori_loop(0, 8, got, 0)
        for which in (1, 0):
            g = tick - (1 - which) * P2_FROM - LAG
            if 0 <= g < KVH:
                give_far(which, g)
            if 0 <= g - LAG < KVH:
                finish(which, g - LAG)
                if which == 1:
                    share(g - LAG)
        for i in range(KVH):
            since = tick - (2 * LAG + i + RS_LATE)
            if since == 0:
                shares[i].wait()
                c0, width, first = GROUPS[i]
                groups[i] = scatter_group(here, xt, dvg, dw_ref, c0, width, first, *scratch[i * 9 : (i + 1) * 9])
            if since in RS_AT[KINDS[i]]:
                next(groups[i], None)
    for which in range(2):
        for g in range(KVH):
            halo_x(which, g).wait_send()
            halo_y(which, g).wait_send()
            back_y(which, g).wait_send()
            back_x(which, g).wait_send()


def fused(lengths, q_rows, k_rows, v_rows, do_rows, x_rows):
    scratch = [
        pltpu.VMEM((1, 64), jnp.int32),
        pltpu.VMEM((256, 4096), BF),
        pltpu.VMEM((256, 4096), BF),
        pltpu.VMEM((256, 4096), BF),
        pltpu.VMEM((KVH, 768, HD), BF),
        pltpu.VMEM((KVH, 768, HD), BF),
        pltpu.VMEM((2, SPAN, GROUP * HALF), F32),
        pltpu.VMEM((KVH, 2, SPAN, GROUP * HALF), BF),
        pltpu.VMEM((768, HD), F32),
        pltpu.VMEM((2, KVH, 256, HD), BF),
        pltpu.VMEM((2, KVH, 256, HD), BF),
        pltpu.VMEM((2, KVH, 256, HD), BF),
        pltpu.VMEM((2, KVH, 256, HD), BF),
        pltpu.VMEM((2, KVH, 256, HD), F32),
        pltpu.VMEM((256, 2048), BF),
        pltpu.VMEM((512, 1024), BF),
        pltpu.VMEM((2, 8, 4, 2, 16, 512), BF),
        pltpu.SemaphoreType.DMA((4,)),
        pltpu.SemaphoreType.DMA((2, KVH)),
        pltpu.SemaphoreType.DMA((2, 8, KVH)),
        pltpu.SemaphoreType.DMA((2, 10)),
    ]
    for _, width, first in GROUPS:
        scratch += group_scratch(width, first)
    vmem, hbm = pl.BlockSpec(memory_space=pltpu.VMEM), pl.BlockSpec(memory_space=pltpu.HBM)
    return pl.pallas_call(
        fused_kernel,
        out_shape=(
            jax.ShapeDtypeStruct((256, 4096), BF),
            jax.ShapeDtypeStruct((256, 1024), BF),
            jax.ShapeDtypeStruct((256, 1024), BF),
            jax.ShapeDtypeStruct((16, 1024), F32),
        ),
        in_specs=[hbm] * 6,
        out_specs=[vmem] * 4,
        scratch_shapes=scratch,
        compiler_params=pltpu.CompilerParams(
            collective_id=1, has_side_effects=True, vmem_limit_bytes=VMEM_MB * 2**20
        ),
        cost_estimate=pl.CostEstimate(flops=10**10, bytes_accessed=12 * 2**20, transcendentals=6 * 10**6),
    )(lengths, q_rows, k_rows, v_rows, do_rows, x_rows)


def store_kernel(*refs):
    copies = [pltpu.make_async_copy(refs[i], refs[4 + i], refs[8].at[i]) for i in range(4)]
    for copy in copies:
        copy.start()
    for copy in copies:
        copy.wait()


def store(outs):
    return pl.pallas_call(
        store_kernel,
        out_shape=tuple(jax.ShapeDtypeStruct(out.shape, out.dtype) for out in outs),
        in_specs=[pl.BlockSpec(memory_space=pl.ANY)] * 4,
        out_specs=[pl.BlockSpec(memory_space=pltpu.HBM)] * 4,
        scratch_shapes=[pltpu.SemaphoreType.DMA((4,))],
        compiler_params=pltpu.CompilerParams(vmem_limit_bytes=2**20),
    )(*outs)


def local(queries, keys, values, out_grad, layer_input, doc_lengths):
    rows = (doc_lengths, queries[0], keys[0], values[0], out_grad[0], layer_input[0])
    outs = store(fused(*[pltpu.with_memory_space_constraint(part, pltpu.HBM) for part in rows]))
    return (outs[0][None], outs[1][None], outs[2][None], outs[3])


def solution(mesh):
    placed = (
        P("dp", "ctx", None),
        P("dp", "ctx", None),
        P("dp", "ctx", None),
        P("dp", "ctx", None),
        P("dp", "ctx", None),
        P("dp", None),
    )
    return jax.shard_map(
        local,
        mesh=mesh,
        in_specs=placed,
        out_specs=(
            P("dp", "ctx", None),
            P("dp", "ctx", None),
            P("dp", "ctx", None),
            P(("dp", "ctx"), None),
        ),
        check_vma=False,
    )
```
